32 devices in a mesh: groups: 2 (over y), sector: 4 (over z), term: 2 (over x), rep: 2 (over core).
Axes of the slice: x: 2, y: 2, z: 4, core: 2. Of those that a mesh axis runs over, the one named last changes fastest.
Arguments:
- wave_block: bfloat16 [16, 512, 512], P(('groups', 'sector'), 'rep', 'term'), parts along dimension 0
- left_env: bfloat16 [24, 16, 512, 512], P('term', ('groups', 'sector'), 'rep'), parts along dimension 1
- right_env: bfloat16 [24, 16, 512, 512], P('term', ('groups', 'sector')), parts along dimension 1
- term_shift: int32 [24], P('term'), may hold values from -1 to 1
- left_sizes: int32 [16], P(('groups', 'sector')), parts along dimension 0, may hold values from 128 to 512, as said below
- right_sizes: int32 [16], P(('groups', 'sector')), parts along dimension 0, may hold values from 128 to 512, as said below
Outputs:
- next_vector: bfloat16 [16, 512, 512], P(('groups', 'sector'), 'rep', 'term'), parts along dimension 0
- coefficients: float32 [12], P('groups'), parts along dimension 0
The draws below stay inside these ranges and needn't reach their ends.
There are 2 independent parts, one for each index of `groups`. The reference program is written for one: setup_inputs(seed, part) draws one part's arguments, and reference() takes and returns one part's arrays. A program takes and returns all parts, laid end to end along the dimension named above; an argument that names none is the same for every part. Nothing has to cross between parts.
Inputs may be any that keep to these rules, and one draw needn't show every extreme that they name: `left_sizes`: one sector has exactly 512 live left states. `right_sizes`: one sector has exactly 512 live right states.
All inputs are finite; a program needn't handle non-finite values.
Results may differ from the reference program's by a relative error of at most 0.013.
Values may be sent and summed in bfloat16 or wider, within the bound.
A program may use at most 64 MiB of HBM per device.

```python
import jax
import jax.numpy as jnp
from jax import lax

BK = 512
W = 24
STEPS = 3
NS = 8


def noise_values(key, shape):
    return jnp.clip(jax.random.normal(key, shape, jnp.float32), -6.0, 6.0)


def rising_blocks(key, ratio):
    positions = jnp.arange(NS, dtype=jnp.float32) / jnp.float32(max(NS - 1, 1))
    amplitude = jnp.exp(positions * jnp.log(jnp.float32(ratio)))
    return noise_values(key, (NS, BK, BK)) * amplitude[:, None, None]


def environment(key):
    random_part = noise_values(key, (W, NS, BK, BK)) / jnp.sqrt(jnp.float32(BK))
    ones_diagonal = jnp.eye(BK, dtype=jnp.float32)
    return (random_part + ones_diagonal[None, None]).astype(jnp.bfloat16)


def draw_wave_block(key, part):
    key = jax.random.fold_in(key, 31)
    values = rising_blocks(key, 2.4494897)
    return values.astype(jnp.bfloat16)


def draw_left_env(key, part):
    key = jax.random.fold_in(key, 41)
    return environment(key)


def draw_right_env(key, part):
    key = jax.random.fold_in(key, 53)
    return environment(key)


def draw_left_sizes(key, part):
    key = jax.random.fold_in(key, 11)
    values = jax.random.randint(key, (NS,), BK // 4, BK + 1)
    chosen = jax.random.randint(jax.random.fold_in(key, 5), (), 0, NS)
    return jnp.where(jnp.arange(NS) == chosen, BK, values).astype(jnp.int32)


def draw_right_sizes(key, part):
    key = jax.random.fold_in(key, 23)
    values = jax.random.randint(key, (NS,), BK // 4, BK + 1)
    chosen = jax.random.randint(jax.random.fold_in(key, 5), (), 0, NS)
    return jnp.where(jnp.arange(NS) == chosen, BK, values).astype(jnp.int32)


def touch_ends(values, rng, smallest, top_value):
    shape = values.shape
    index_at = [jax.random.randint(jax.random.fold_in(rng, axis), (), 0, shape[axis]) for axis in range(len(shape))]
    values = values.at[tuple(index_at)].set(smallest)
    longest = shape.index(max(shape))
    index_at[longest] = (index_at[longest] + 1) % shape[longest]
    return values.at[tuple(index_at)].set(top_value)


def setup_inputs(seed: int = 0, part: int = 0) -> dict:
    seeds = jax.random.split(jax.random.key(seed), 7)
    own_keys = jax.random.split(jax.random.fold_in(seeds[6], part), 7)
    return {
        "wave_block": draw_wave_block(jax.random.fold_in(jax.random.fold_in(seeds[6], part), 71), part),
        "left_env": draw_left_env(jax.random.fold_in(jax.random.fold_in(seeds[6], part), 71), part),
        "right_env": draw_right_env(jax.random.fold_in(jax.random.fold_in(seeds[6], part), 71), part),
        "term_shift": touch_ends(jax.random.randint(seeds[3], (W,), -1, 2), jax.random.fold_in(seeds[3], 1), -1, 1).astype(jnp.int32),
        "left_sizes": draw_left_sizes(jax.random.fold_in(jax.random.fold_in(seeds[6], part), 71), part),
        "right_sizes": draw_right_sizes(jax.random.fold_in(jax.random.fold_in(seeds[6], part), 71), part),
    }


def apply_operator(vector, left_env, right_env, term_shift, occupied):
    extended = jnp.pad(vector, ((1, 1), (0, 0), (0, 0)))
    from_below = extended[:-2]
    from_same = extended[1:-1]
    from_above = extended[2:]

    def one_term(running, packed):
        left_one, right_one, shifts = packed
        source = jnp.where(shifts == 1, from_below, jnp.where(shifts == 0, from_same, from_above))
        partial_value = jnp.einsum('jrk,jkc->jrc', left_one.astype(jnp.float32), source.astype(jnp.float32)).astype(jnp.bfloat16)
        running = running + jnp.einsum('jrc,jce->jre', partial_value.astype(jnp.float32), right_one.astype(jnp.float32))
        return (running, None)
    empty = jnp.zeros(vector.shape, jnp.float32)
    summed, _ = lax.scan(one_term, empty, (left_env, right_env, term_shift))
    return jnp.where(occupied, summed, jnp.float32(0.0))

def reference(wave_block, left_env, right_env, term_shift, left_sizes, right_sizes):
    row_ids = jnp.arange(BK, dtype=jnp.int32)
    occupied = (row_ids[None, :, None] < left_sizes[:, None, None]) & (row_ids[None, None, :] < right_sizes[:, None, None])
    entries = jnp.float32(NS * BK * BK)
    masked_start = jnp.where(occupied, wave_block.astype(jnp.float32), jnp.float32(0.0))
    start_scale = jnp.sqrt(jnp.sum(masked_start * masked_start) / entries + 1e-06)
    vector = (masked_start / start_scale).astype(jnp.bfloat16)
    previous = jnp.zeros(vector.shape, jnp.bfloat16)
    beta_now = jnp.float32(0.0)
    alphas = []
    betas = []
    for number in range(STEPS):
        image_now = apply_operator(vector, left_env, right_env, term_shift, occupied)
        alpha_now = jnp.sum(vector.astype(jnp.float32) * image_now) / entries
        residual = image_now - alpha_now * vector.astype(jnp.float32) - beta_now * previous.astype(jnp.float32)
        beta_now = jnp.sqrt(jnp.sum(residual * residual) / entries + 1e-06)
        previous = vector
        vector = (residual / beta_now).astype(jnp.bfloat16)
        alphas.append(alpha_now)
        betas.append(beta_now)
    return (vector, jnp.stack(alphas + betas).astype(jnp.float32))
```

```python
import functools

import jax
import jax.numpy as jnp
from jax import lax
from jax.experimental import pallas as pl
from jax.experimental.pallas import tpu as pltpu
from jax.sharding import PartitionSpec as P

STEPS = 3
MESH_ID = pl.DeviceIdType.MESH


def largest_divisor(count, limit):
    return max(d for d in range(1, limit + 1) if count % d == 0)


def kernel(
    sectors_n, terms_n, reps_n,
    shift_ref, left_size_ref, right_size_ref, wave_ref, left_hbm, right_hbm,
    out_ref, coef_ref,
    left, right, vec, part, acc, share_out, share_in, red,
    load_sem, x_send, piece_recv, z_send, core_send, core_recv,
    share_send, share_recv, red_send, red_recv,
):
    local_n, rows, cols = wave_ref.shape
    width = left.shape[3]
    terms_local = left.shape[1]
    peers = sectors_n * terms_n * reps_n
    entries = jnp.float32(local_n * sectors_n * width * width)
    z = lax.axis_index("sector")
    x = lax.axis_index("term")
    c = lax.axis_index("rep")
    me = (z * terms_n + x) * reps_n + c
    not_first = z > 0
    not_last = z < sectors_n - 1
    row0 = pl.multiple_of(c * rows, rows)
    other_row0 = pl.multiple_of((1 - c) * rows, rows)

    def place(number):
        return {
            "sector": number // (terms_n * reps_n),
            "term": (number // reps_n) % terms_n,
            "rep": number % reps_n,
        }

    def side(offset):
        return lax.rem(x + offset, terms_n)

    loads = []
    for j in range(local_n):
        loads.append((
            pltpu.make_async_copy(left_hbm.at[:, j], left.at[j], load_sem.at[j, 0]),
            pltpu.make_async_copy(right_hbm.at[:, j], right.at[j], load_sem.at[j, 1]),
        ))
    for pair in loads:
        for copy in pair:
            copy.start()

    barrier = pltpu.get_barrier_semaphore()

    def greet(i, carry):
        pl.semaphore_signal(
            barrier, inc=1, device_id=place(lax.rem(me + i, peers)), device_id_type=MESH_ID
        )
        return carry

    lax.fori_loop(1, peers, greet, 0)

    def fold(values):
        row = jnp.sum(values, axis=0, keepdims=True)
        return sum(row[:, i : i + 128] for i in range(0, row.shape[1], 128))

    def share_sum(slot, row):
        red[slot, me] = row

        def send(i, carry):
            pltpu.make_async_remote_copy(
                src_ref=red.at[slot, me], dst_ref=red.at[slot, me],
                send_sem=red_send.at[slot], recv_sem=red_recv.at[slot],
                device_id=place(lax.rem(me + i, peers)), device_id_type=MESH_ID,
            ).start()
            return carry

        lax.fori_loop(1, peers, send, 0)

    def whole_sum(slot):
        pltpu.make_async_remote_copy(
            src_ref=red.at[slot, pl.ds(0, peers - 1)], dst_ref=red.at[slot, pl.ds(0, peers - 1)],
            send_sem=red_send.at[slot], recv_sem=red_recv.at[slot],
            device_id=place(lax.rem(me + 1, peers)), device_id_type=MESH_ID,
        ).wait()
        return jnp.sum(jnp.sum(red[slot], axis=0), axis=1, keepdims=True) / entries

    def piece(k, s, t):
        return vec.at[k, s, t, pl.ds(row0, rows)]

    def x_copy(k, j, offset, source):
        return pltpu.make_async_remote_copy(
            src_ref=piece(k, 1 + j, source), dst_ref=piece(k, 1 + j, source),
            send_sem=x_send.at[k, j, offset], recv_sem=piece_recv.at[k, 1 + j, source],
            device_id={"term": side(offset)}, device_id_type=MESH_ID,
        )

    def z_copy(k, up, t):
        src = piece(k, local_n if up else 1, t)
        s = 0 if up else local_n + 1
        target = lax.rem(z + (1 if up else sectors_n - 1), sectors_n)
        return pltpu.make_async_remote_copy(
            src_ref=src, dst_ref=piece(k, s, t),
            send_sem=z_send.at[k, int(up), t], recv_sem=piece_recv.at[k, s, t],
            device_id={"sector": target}, device_id_type=MESH_ID,
        )

    def core_copy(k, s, t, start=row0):
        ref = vec.at[k, s, t, pl.ds(start, rows)]
        return pltpu.make_async_remote_copy(
            src_ref=ref, dst_ref=ref,
            send_sem=core_send.at[k, s, t], recv_sem=core_recv.at[k, s, t],
            device_id={"rep": 1 - c}, device_id_type=MESH_ID,
        )

    def send_along_z(k, j, t):
        if sectors_n > 1 and j == 0:
            @pl.when(not_first)
            def _():
                z_copy(k, False, t).start()
        if sectors_n > 1 and j == local_n - 1:
            @pl.when(not_last)
            def _():
                z_copy(k, True, t).start()

    def send_own(k, j):
        for offset in range(1, terms_n):
            x_copy(k, j, offset, x).start()
        send_along_z(k, j, x)
        core_copy(k, 1 + j, x).start()

    edges = ((0, True, not_first), (local_n + 1, False, not_last)) if sectors_n > 1 else ()

    def gather_rest(k):
        for j in range(local_n):
            for offset in range(1, terms_n):
                t = side(offset)
                x_copy(k, j, offset, t).wait_recv()
                send_along_z(k, j, t)
                core_copy(k, 1 + j, t).start()
        for offset in range(terms_n):
            t = side(offset)
            for s, up, there in edges:
                @pl.when(there)
                def _():
                    z_copy(k, up, t).wait_recv()
                    core_copy(k, s, t).start()
        for j in range(local_n):
            for t in range(terms_n):
                core_copy(k, 1 + j, t, other_row0).wait_recv()
        for s, up, there in edges:
            @pl.when(there)
            def _():
                for t in range(terms_n):
                    core_copy(k, s, t, other_row0).wait_recv()

    def drain(k):
        for j in range(local_n):
            for offset in range(1, terms_n):
                x_copy(k, j, offset, x).wait_send()
            for t in range(terms_n):
                core_copy(k, 1 + j, t).wait_send()
        for s, up, there in edges:
            @pl.when(there)
            def _():
                for t in range(terms_n):
                    core_copy(k, s, t).wait_send()
                    z_copy(k, not up, t).wait_send()

    def share_copy(k, j, offset):
        return pltpu.make_async_remote_copy(
            src_ref=share_out.at[j, offset], dst_ref=share_in.at[k, j, terms_n - offset],
            send_sem=share_send.at[k, j, offset], recv_sem=share_recv.at[k, j, terms_n - offset],
            device_id={"term": side(offset)}, device_id_type=MESH_ID,
        )

    def first_products(k, j):
        def body(w, carry):
            s = j + 1 - shift_ref[w]
            for t in range(terms_n):
                at = pl.multiple_of(w * width + t * cols, cols)
                part[j, :, pl.ds(at, cols)] = jnp.dot(
                    left[j, w], vec[k, s, t], preferred_element_type=jnp.float32
                ).astype(jnp.bfloat16)
            return carry

        lax.fori_loop(0, terms_local, body, 0)

    group = largest_divisor(terms_local, 4)

    def second_products(j, offset):
        col0 = pl.multiple_of(side(offset) * cols, cols)
        depth = group * width

        def product(g):
            at = pl.multiple_of(g * depth, depth)
            env = right[j, pl.ds(g * group, group), :, pl.ds(col0, cols)]
            return jnp.dot(
                part[j, :, pl.ds(at, depth)], env.reshape(depth, cols),
                preferred_element_type=jnp.float32,
            )

        acc[j, offset] = jnp.zeros((rows, cols), jnp.float32)

        def body(g, carry):
            acc[j, offset] += product(g)
            return carry

        lax.fori_loop(0, terms_local // group, body, 0)

    def own(k, j):
        return vec[k, 1 + j, x, pl.ds(row0, rows)].astype(jnp.float32)

    row_ids = row0 + lax.broadcasted_iota(jnp.int32, (rows, cols), 0)
    col_ids = x * cols + lax.broadcasted_iota(jnp.int32, (rows, cols), 1)

    def occupied(j):
        return (row_ids < left_size_ref[j]) & (col_ids < right_size_ref[j])

    squares = jnp.zeros((1, 128), jnp.float32)
    for j in range(local_n):
        start = jnp.where(occupied(j), wave_ref[j].astype(jnp.float32), 0.0)
        vec[0, 1 + j, x, pl.ds(row0, rows)] = start.astype(jnp.bfloat16)
        squares += fold(start * start)

    pl.semaphore_wait(barrier, peers - 1)
    for j in range(local_n):
        send_own(0, j)
    share_sum(0, squares)

    def clear(k, s):
        for t in range(terms_n):
            vec[k, s, t] = jnp.zeros((width, cols), jnp.bfloat16)

    @pl.when(jnp.logical_not(not_first))
    def _():
        for k in range(STEPS):
            clear(k, 0)

    @pl.when(jnp.logical_not(not_last))
    def _():
        for k in range(STEPS):
            clear(k, local_n + 1)

    alphas, norms, inverse = [], [], []
    for k in range(STEPS):
        gather_rest(k)
        for j in range(local_n):
            if k == 0:
                loads[j][0].wait()
            first_products(k, j)
            if k == 0:
                loads[j][1].wait()
            for offset in range(1, terms_n):
                second_products(j, offset)
                share_out[j, offset] = acc[j, offset].astype(jnp.bfloat16)
                share_copy(k, j, offset).start()
        for j in range(local_n):
            second_products(j, 0)
        norm = jnp.sqrt(whole_sum(2 * k) + 1e-06)
        scale = 1.0 / norm
        norms.append(norm)
        inverse.append(scale)
        overlap = jnp.zeros((1, 128), jnp.float32)
        for j in range(local_n):
            for offset in range(terms_n):
                held = vec[k, 1 + j, side(offset), pl.ds(row0, rows)].astype(jnp.float32)
                overlap += fold((held * scale) * (acc[j, offset] * scale))
        share_sum(2 * k + 1, overlap)
        drain(k)
        alpha = whole_sum(2 * k + 1)
        alphas.append(alpha)
        squares = jnp.zeros((1, 128), jnp.float32)
        for j in range(local_n):
            image = acc[j, 0]
            for offset in range(1, terms_n):
                share_copy(k, j, terms_n - offset).wait_recv()
                image += share_in[k, j, offset].astype(jnp.float32)
            residual = jnp.where(occupied(j), image * scale, 0.0) - (alpha * scale) * own(k, j)
            if k > 0:
                residual -= (norm * inverse[k - 1]) * own(k - 1, j)
            if k < STEPS - 1:
                vec[k + 1, 1 + j, x, pl.ds(row0, rows)] = residual.astype(jnp.bfloat16)
                send_own(k + 1, j)
            else:
                acc[j, 0] = residual
            squares += fold(residual * residual)
        share_sum(2 * k + 2, squares)
        for j in range(local_n):
            for offset in range(1, terms_n):
                share_copy(k, j, offset).wait_send()
    norm = jnp.sqrt(whole_sum(2 * STEPS) + 1e-06)
    norms.append(norm)
    scale = 1.0 / norm
    for j in range(local_n):
        out_ref[j] = (acc[j, 0] * scale).astype(jnp.bfloat16)
    lanes = lax.broadcasted_iota(jnp.int32, (1, 128), 1)
    row = jnp.zeros((1, 128), jnp.float32)
    for i, value in enumerate(alphas + norms[1:]):
        row = jnp.where(lanes == i, value, row)
    coef_ref[...] = row[:, : 2 * STEPS]


def on_device(sizes, wave_block, left_env, right_env, term_shift, left_sizes, right_sizes):
    local_n, rows, cols = wave_block.shape
    terms_local, _, _, width = left_env.shape
    sectors_n, terms_n, reps_n = sizes
    peers = sectors_n * terms_n * reps_n
    slots = local_n + 2
    dma = pltpu.SemaphoreType.DMA
    smem = pl.BlockSpec(memory_space=pltpu.SMEM)
    vmem = pl.BlockSpec(memory_space=pltpu.VMEM)
    hbm = pl.BlockSpec(memory_space=pl.ANY)
    bf16, f32 = jnp.bfloat16, jnp.float32
    vector, coefficients = pl.pallas_call(
        functools.partial(kernel, sectors_n, terms_n, reps_n),
        out_shape=(
            jax.ShapeDtypeStruct((local_n, rows, cols), bf16),
            jax.ShapeDtypeStruct((1, 2 * STEPS), f32),
        ),
        in_specs=[smem, smem, smem, vmem, hbm, hbm],
        out_specs=(vmem, vmem),
        scratch_shapes=[
            pltpu.VMEM((local_n, terms_local, rows, width), bf16),
            pltpu.VMEM((local_n, terms_local, width, width), bf16),
            pltpu.VMEM((STEPS, slots, terms_n, width, cols), bf16),
            pltpu.VMEM((local_n, rows, terms_local * width), bf16),
            pltpu.VMEM((local_n, terms_n, rows, cols), f32),
            pltpu.VMEM((local_n, terms_n, rows, cols), bf16),
            pltpu.VMEM((STEPS, local_n, terms_n, rows, cols), bf16),
            pltpu.VMEM((2 * STEPS + 1, peers, 1, 128), f32),
            dma((local_n, 2)),
            dma((STEPS, local_n, terms_n)),
            dma((STEPS, slots, terms_n)),
            dma((STEPS, 2, terms_n)),
            dma((STEPS, slots, terms_n)),
            dma((STEPS, slots, terms_n)),
            dma((STEPS, local_n, terms_n)),
            dma((STEPS, local_n, terms_n)),
            dma((2 * STEPS + 1,)),
            dma((2 * STEPS + 1,)),
        ],
        compiler_params=pltpu.CompilerParams(
            collective_id=0, has_side_effects=True, vmem_limit_bytes=56 * 1024 * 1024
        ),
    )(term_shift, left_sizes, right_sizes, wave_block, left_env, right_env)
    return vector, coefficients.reshape(2 * STEPS)


def solution(mesh):
    in_specs = (
        P(("groups", "sector"), "rep", "term"),
        P("term", ("groups", "sector"), "rep", None),
        P("term", ("groups", "sector"), None, None),
        P("term"),
        P(("groups", "sector")),
        P(("groups", "sector")),
    )
    out_specs = (P(("groups", "sector"), "rep", "term"), P("groups"))
    sizes = (mesh.shape["sector"], mesh.shape["term"], mesh.shape["rep"])
    return jax.shard_map(
        functools.partial(on_device, sizes), mesh=mesh, in_specs=in_specs, out_specs=out_specs,
        check_vma=False,
    )
```

```python
import functools

import jax
import jax.numpy as jnp
from jax import lax
from jax.experimental import pallas as pl
from jax.experimental.pallas import tpu as pltpu
from jax.sharding import PartitionSpec as P

STEPS = 3
CHUNKS = 2
UNROLL = 2
MESH_ID = pl.DeviceIdType.MESH


def largest_divisor(count, limit):
    return max(d for d in range(1, limit + 1) if count % d == 0)


def kernel(
    sectors_n, terms_n, reps_n,
    shift_ref, left_size_ref, right_size_ref, wave_ref, left_hbm, right_hbm,
    out_ref, coef_ref,
    left, right, near, far, part, acc, share_out, share_in, red,
    load_sem, x_send, piece_recv, z_send, core_send, core_recv,
    share_send, share_recv, red_send, red_recv,
):
    local_n, rows, cols = wave_ref.shape
    width = left.shape[3]
    terms_local = left.shape[1]
    peers = sectors_n * terms_n * reps_n
    entries = jnp.float32(local_n * sectors_n * width * width)
    z = lax.axis_index("sector")
    x = lax.axis_index("term")
    c = lax.axis_index("rep")
    me = (z * terms_n + x) * reps_n + c
    not_first = z > 0
    not_last = z < sectors_n - 1
    row0 = pl.multiple_of(c * rows, rows)
    height = rows // CHUNKS

    def place(number):
        return {
            "sector": number // (terms_n * reps_n),
            "term": (number // reps_n) % terms_n,
            "rep": number % reps_n,
        }

    def side(offset):
        return lax.rem(x + offset, terms_n)

    loads = []
    for j in range(local_n):
        loads.append((
            pltpu.make_async_copy(left_hbm.at[:, j], left.at[j], load_sem.at[j, 0]),
            pltpu.make_async_copy(right_hbm.at[:, j], right.at[j], load_sem.at[j, 1]),
        ))
    for pair in loads:
        for copy in pair:
            copy.start()

    barrier = pltpu.get_barrier_semaphore()

    def greet(i, carry):
        pl.semaphore_signal(
            barrier, inc=1, device_id=place(lax.rem(me + i, peers)), device_id_type=MESH_ID
        )
        return carry

    lax.fori_loop(1, peers, greet, 0)

    def fold(values):
        row = jnp.sum(values, axis=0, keepdims=True)
        return sum(row[:, i : i + 128] for i in range(0, row.shape[1], 128))

    def share_sum(slot, row):
        red[slot, me] = row

        def send(i, carry):
            pltpu.make_async_remote_copy(
                src_ref=red.at[slot, me], dst_ref=red.at[slot, me],
                send_sem=red_send.at[slot], recv_sem=red_recv.at[slot],
                device_id=place(lax.rem(me + i, peers)), device_id_type=MESH_ID,
            ).start()
            return carry

        lax.fori_loop(1, peers, send, 0)

    def whole_sum(slot):
        pltpu.make_async_remote_copy(
            src_ref=red.at[slot, pl.ds(0, peers - 1)], dst_ref=red.at[slot, pl.ds(0, peers - 1)],
            send_sem=red_send.at[slot], recv_sem=red_recv.at[slot],
            device_id=place(lax.rem(me + 1, peers)), device_id_type=MESH_ID,
        ).wait()
        return jnp.sum(jnp.sum(red[slot], axis=0), axis=1, keepdims=True) / entries

    def chunk(k, s, offset, q, core):
        at = pl.ds(pl.multiple_of(core * rows + q * height, height), height)
        return near.at[k, s, at] if offset == 0 else far.at[k, s, offset - 1, at]

    def x_copy(k, j, offset, q):
        return pltpu.make_async_remote_copy(
            src_ref=chunk(k, 1 + j, 0, q, c), dst_ref=chunk(k, 1 + j, terms_n - offset, q, c),
            send_sem=x_send.at[k, j, offset, q],
            recv_sem=piece_recv.at[k, 1 + j, terms_n - offset, q],
            device_id={"term": side(offset)}, device_id_type=MESH_ID,
        )

    def z_copy(k, up, offset, q):
        s = 0 if up else local_n + 1
        target = lax.rem(z + (1 if up else sectors_n - 1), sectors_n)
        return pltpu.make_async_remote_copy(
            src_ref=chunk(k, local_n if up else 1, offset, q, c),
            dst_ref=chunk(k, s, offset, q, c),
            send_sem=z_send.at[k, int(up), offset, q], recv_sem=piece_recv.at[k, s, offset, q],
            device_id={"sector": target}, device_id_type=MESH_ID,
        )

    def core_copy(k, s, offset, q, core=c):
        ref = chunk(k, s, offset, q, core)
        return pltpu.make_async_remote_copy(
            src_ref=ref, dst_ref=ref,
            send_sem=core_send.at[k, s, offset, q], recv_sem=core_recv.at[k, s, offset, q],
            device_id={"rep": 1 - c}, device_id_type=MESH_ID,
        )

    def send_along_z(k, j, offset, q):
        if sectors_n > 1 and j == 0:
            @pl.when(not_first)
            def _():
                z_copy(k, False, offset, q).start()
        if sectors_n > 1 and j == local_n - 1:
            @pl.when(not_last)
            def _():
                z_copy(k, True, offset, q).start()

    def send_own(k, j):
        for q in range(CHUNKS):
            for offset in range(1, terms_n):
                x_copy(k, j, offset, q).start()
            send_along_z(k, j, 0, q)
            core_copy(k, 1 + j, 0, q).start()

    def pass_on(k, j):
        for q in range(CHUNKS):
            for offset in range(1, terms_n):
                x_copy(k, j, terms_n - offset, q).wait_recv()
                send_along_z(k, j, offset, q)
                core_copy(k, 1 + j, offset, q).start()

    edges = ((0, True, not_first), (local_n + 1, False, not_last)) if sectors_n > 1 else ()

    def pass_edges(k, offset):
        for q in range(CHUNKS):
            for s, up, there in edges:
                @pl.when(there)
                def _():
                    z_copy(k, up, offset, q).wait_recv()
                    core_copy(k, s, offset, q).start()

    def arrive(k, offset):
        for q in range(CHUNKS):
            for j in range(local_n):
                core_copy(k, 1 + j, offset, q, 1 - c).wait_recv()
            for s, up, there in edges:
                @pl.when(there)
                def _():
                    core_copy(k, s, offset, q, 1 - c).wait_recv()

    def drain(k):
        for q in range(CHUNKS):
            for j in range(local_n):
                for offset in range(1, terms_n):
                    x_copy(k, j, offset, q).wait_send()
                for offset in range(terms_n):
                    core_copy(k, 1 + j, offset, q).wait_send()
            for s, up, there in edges:
                @pl.when(there)
                def _():
                    for offset in range(terms_n):
                        core_copy(k, s, offset, q).wait_send()
                        z_copy(k, not up, offset, q).wait_send()

    def share_copy(k, j, offset):
        return pltpu.make_async_remote_copy(
            src_ref=share_out.at[j, offset], dst_ref=share_in.at[k, j, terms_n - offset],
            send_sem=share_send.at[k, j, offset], recv_sem=share_recv.at[k, j, terms_n - offset],
            device_id={"term": side(offset)}, device_id_type=MESH_ID,
        )

    def first_products(k, j, offset):
        col0 = side(offset) * cols

        def body(w, carry):
            s = j + 1 - shift_ref[w]
            source = near[k, s] if offset == 0 else far[k, s, offset - 1]
            at = pl.multiple_of(w * width + col0, cols)
            part[j, :, pl.ds(at, cols)] = jnp.dot(
                left[j, w], source, preferred_element_type=jnp.float32
            ).astype(jnp.bfloat16)
            return carry

        lax.fori_loop(0, terms_local, body, 0, unroll=largest_divisor(terms_local, UNROLL))

    group = largest_divisor(terms_local, 4)

    def second_products(j, offset):
        col0 = pl.multiple_of(side(offset) * cols, cols)
        depth = group * width

        def product(g):
            at = pl.multiple_of(g * depth, depth)
            env = right[j, pl.ds(g * group, group), :, pl.ds(col0, cols)]
            return jnp.dot(
                part[j, :, pl.ds(at, depth)], env.reshape(depth, cols),
                preferred_element_type=jnp.float32,
            )

        acc[j, offset] = jnp.zeros((rows, cols), jnp.float32)

        def body(g, carry):
            acc[j, offset] += product(g)
            return carry

        lax.fori_loop(0, terms_local // group, body, 0)

    def own(k, j):
        return near[k, 1 + j, pl.ds(row0, rows)].astype(jnp.float32)

    row_ids = row0 + lax.broadcasted_iota(jnp.int32, (rows, cols), 0)
    col_ids = x * cols + lax.broadcasted_iota(jnp.int32, (rows, cols), 1)

    def occupied(j):
        return (row_ids < left_size_ref[j]) & (col_ids < right_size_ref[j])

    squares = jnp.zeros((1, 128), jnp.float32)
    for j in range(local_n):
        start = jnp.where(occupied(j), wave_ref[j].astype(jnp.float32), 0.0)
        near[0, 1 + j, pl.ds(row0, rows)] = start.astype(jnp.bfloat16)
        squares += fold(start * start)

    pl.semaphore_wait(barrier, peers - 1)
    for j in range(local_n):
        send_own(0, j)
    share_sum(0, squares)

    def clear(k, s):
        near[k, s] = jnp.zeros((width, cols), jnp.bfloat16)
        far[k, s] = jnp.zeros(far.shape[2:], jnp.bfloat16)

    @pl.when(jnp.logical_not(not_first))
    def _():
        for k in range(STEPS):
            clear(k, 0)

    @pl.when(jnp.logical_not(not_last))
    def _():
        for k in range(STEPS):
            clear(k, local_n + 1)

    alphas, norms, inverse = [], [], []
    for k in range(STEPS):
        pass_on(k, 0)
        pass_edges(k, 0)
        arrive(k, 0)
        for j in range(local_n):
            if k == 0:
                loads[j][0].wait()
            first_products(k, j, 0)
            if j < local_n - 1:
                pass_on(k, j + 1)
        for offset in range(1, terms_n):
            pass_edges(k, offset)
        for offset in range(1, terms_n):
            arrive(k, offset)
        for j in range(local_n):
            for offset in range(1, terms_n):
                first_products(k, j, offset)
            if k == 0:
                loads[j][1].wait()
            for offset in range(1, terms_n):
                second_products(j, offset)
                share_out[j, offset] = acc[j, offset].astype(jnp.bfloat16)
                share_copy(k, j, offset).start()
        for j in range(local_n):
            second_products(j, 0)
        norm = jnp.sqrt(whole_sum(2 * k) + 1e-06)
        scale = 1.0 / norm
        norms.append(norm)
        inverse.append(scale)
        overlap = jnp.zeros((1, 128), jnp.float32)
        for j in range(local_n):
            for offset in range(terms_n):
                mine = pl.ds(row0, rows)
                held = near[k, 1 + j, mine] if offset == 0 else far[k, 1 + j, offset - 1, mine]
                held = held.astype(jnp.float32)
                overlap += fold((held * scale) * (acc[j, offset] * scale))
        share_sum(2 * k + 1, overlap)
        drain(k)
        alpha = whole_sum(2 * k + 1)
        alphas.append(alpha)
        squares = jnp.zeros((1, 128), jnp.float32)
        for j in range(local_n):
            image = acc[j, 0]
            for offset in range(1, terms_n):
                share_copy(k, j, terms_n - offset).wait_recv()
                image += share_in[k, j, offset].astype(jnp.float32)
            residual = jnp.where(occupied(j), image * scale, 0.0) - (alpha * scale) * own(k, j)
            if k > 0:
                residual -= (norm * inverse[k - 1]) * own(k - 1, j)
            if k < STEPS - 1:
                near[k + 1, 1 + j, pl.ds(row0, rows)] = residual.astype(jnp.bfloat16)
                send_own(k + 1, j)
            else:
                acc[j, 0] = residual
            squares += fold(residual * residual)
        share_sum(2 * k + 2, squares)
        for j in range(local_n):
            for offset in range(1, terms_n):
                share_copy(k, j, offset).wait_send()
    norm = jnp.sqrt(whole_sum(2 * STEPS) + 1e-06)
    norms.append(norm)
    scale = 1.0 / norm
    for j in range(local_n):
        out_ref[j] = (acc[j, 0] * scale).astype(jnp.bfloat16)
    lanes = lax.broadcasted_iota(jnp.int32, (1, 128), 1)
    row = jnp.zeros((1, 128), jnp.float32)
    for i, value in enumerate(alphas + norms[1:]):
        row = jnp.where(lanes == i, value, row)
    coef_ref[...] = row[:, : 2 * STEPS]


def on_device(sizes, wave_block, left_env, right_env, term_shift, left_sizes, right_sizes):
    local_n, rows, cols = wave_block.shape
    terms_local, _, _, width = left_env.shape
    sectors_n, terms_n, reps_n = sizes
    peers = sectors_n * terms_n * reps_n
    slots = local_n + 2
    dma = pltpu.SemaphoreType.DMA
    smem = pl.BlockSpec(memory_space=pltpu.SMEM)
    vmem = pl.BlockSpec(memory_space=pltpu.VMEM)
    hbm = pl.BlockSpec(memory_space=pl.ANY)
    bf16, f32 = jnp.bfloat16, jnp.float32
    vector, coefficients = pl.pallas_call(
        functools.partial(kernel, sectors_n, terms_n, reps_n),
        out_shape=(
            jax.ShapeDtypeStruct((local_n, rows, cols), bf16),
            jax.ShapeDtypeStruct((1, 2 * STEPS), f32),
        ),
        in_specs=[smem, smem, smem, vmem, hbm, hbm],
        out_specs=(vmem, vmem),
        scratch_shapes=[
            pltpu.VMEM((local_n, terms_local, rows, width), bf16),
            pltpu.VMEM((local_n, terms_local, width, width), bf16),
            pltpu.VMEM((STEPS, slots, width, cols), bf16),
            pltpu.VMEM((STEPS, slots, terms_n - 1, width, cols), bf16),
            pltpu.VMEM((local_n, rows, terms_local * width), bf16),
            pltpu.VMEM((local_n, terms_n, rows, cols), f32),
            pltpu.VMEM((local_n, terms_n, rows, cols), bf16),
            pltpu.VMEM((STEPS, local_n, terms_n, rows, cols), bf16),
            pltpu.VMEM((2 * STEPS + 1, peers, 1, 128), f32),
            dma((local_n, 2)),
            dma((STEPS, local_n, terms_n, CHUNKS)),
            dma((STEPS, slots, terms_n, CHUNKS)),
            dma((STEPS, 2, terms_n, CHUNKS)),
            dma((STEPS, slots, terms_n, CHUNKS)),
            dma((STEPS, slots, terms_n, CHUNKS)),
            dma((STEPS, local_n, terms_n)),
            dma((STEPS, local_n, terms_n)),
            dma((2 * STEPS + 1,)),
            dma((2 * STEPS + 1,)),
        ],
        compiler_params=pltpu.CompilerParams(
            collective_id=0, has_side_effects=True, vmem_limit_bytes=56 * 1024 * 1024
        ),
    )(term_shift, left_sizes, right_sizes, wave_block, left_env, right_env)
    return vector, coefficients.reshape(2 * STEPS)


def solution(mesh):
    in_specs = (
        P(("groups", "sector"), "rep", "term"),
        P("term", ("groups", "sector"), "rep", None),
        P("term", ("groups", "sector"), None, None),
        P("term"),
        P(("groups", "sector")),
        P(("groups", "sector")),
    )
    out_specs = (P(("groups", "sector"), "rep", "term"), P("groups"))
    sizes = (mesh.shape["sector"], mesh.shape["term"], mesh.shape["rep"])
    return jax.shard_map(
        functools.partial(on_device, sizes), mesh=mesh, in_specs=in_specs, out_specs=out_specs,
        check_vma=False,
    )
```
